128 devices in a mesh: row: 16 (over x, z_lo, core), col: 8 (over y, z_hi).
Axes of the slice: x: 4, y: 4, z: 4 (z_hi: 2, z_lo: 2; z = z_hi * 2 + z_lo), core: 2. Of those that a mesh axis runs over, the one named last changes fastest.
Arguments:
- pair_rep: bfloat16 [768, 768, 256], P('row', 'col'), may hold values from -6 to 6
- single_rep: bfloat16 [768, 768], replicated, may hold values from -6 to 6
- length: int32 [1], replicated, may hold values from 384 to 768
- pair_gain: float32 [256], replicated, may hold values from 0.25 to 1.75
- pair_proj: bfloat16 [4, 256, 256], replicated, may hold values from -0.375 to 0.375
- bias_weight: bfloat16 [256, 8], replicated, may hold values from -12 to 12
- pair_out_weight: bfloat16 [256, 256], replicated, may hold values from -1 to 1
- single_gain: float32 [768], replicated, may hold values from 0.25 to 1.75
- single_proj: bfloat16 [4, 768, 768], P(None, None, 'col'), may hold values from -0.21875 to 0.21875
- bias_norm_gain: float32 [256], replicated, may hold values from 0.25 to 1.75
- single_bias_weight: bfloat16 [256, 16], replicated, may hold values from -12 to 12
- single_out_weight: bfloat16 [768, 768], P('col'), may hold values from -0.625 to 0.625
Outputs:
- pair_out: bfloat16 [768, 768, 256], P('row', 'col')
- single_out: bfloat16 [768, 768], P('row', 'col')
The draws below stay inside these ranges and needn't reach their ends.
Inputs may be any that keep to these rules, and one draw needn't show every extreme that they name: Positions from length[0] on are padding and never serve as keys.
All inputs are finite; a program needn't handle non-finite values.
Results may differ from the reference program's by a relative error of at most 0.019.
Values may be sent and summed in bfloat16 or wider, within the bound.
No kernel may reach another device: no remote copies, remote signals or barrier semaphores. Data moves between devices by JAX's collectives and lax.ppermute only.
A program may use at most 128 MiB of HBM per device.

```python
import math
import jax
import jax.numpy as jnp
from jax import lax

TOKENS = 768
PAIR_DIM = 256
PAIR_HEADS = 8
PAIR_HEAD_DIM = 32
SINGLE_DIM = 768
SINGLE_HEADS = 16
SINGLE_HEAD_DIM = 48


def draw_bias_weight(key, part):
    base = jax.random.normal(jax.random.fold_in(key, 11), (PAIR_DIM, PAIR_HEADS), jnp.float32) / math.sqrt(PAIR_DIM)
    return jnp.clip(base, -12.0, 12.0).astype(jnp.bfloat16)


def draw_single_bias_weight(key, part):
    base = jax.random.normal(jax.random.fold_in(key, 23), (PAIR_DIM, SINGLE_HEADS), jnp.float32) / math.sqrt(PAIR_DIM)
    return jnp.clip(base, -12.0, 12.0).astype(jnp.bfloat16)


def level_of(key, extent, shards, least, top_value):
    gain = 1.0
    for dim, shards_of in shards:
        heights = jax.random.uniform(jax.random.fold_in(jax.random.fold_in(key, 6), dim), (shards_of,), jnp.float32, least / len(shards), top_value / len(shards))
        gain = gain * jnp.repeat(jnp.exp(heights), extent[dim] // shards_of).reshape((-1,) + (1,) * (len(extent) - 1 - dim))
    return gain


def normal_values(own_key, extent, scale, bound, pieces=(), held_as=jnp.bfloat16):
    entries = jax.random.normal(own_key, extent, jnp.float32) * scale
    if len(pieces) > 0:
        entries = level_of(own_key, extent, pieces, -0.22, 0.18) * entries
    return jnp.clip(entries, min=-bound, max=bound).astype(held_as)


def setup_inputs(seed: int = 0) -> dict:
    splits = jax.random.split(jax.random.key(seed), 13)
    return {
        "pair_rep": normal_values(splits[0], (TOKENS, TOKENS, PAIR_DIM), 1.0, 6.0, ((0, 16), (1, 8))),
        "single_rep": normal_values(splits[1], (TOKENS, SINGLE_DIM), 1.0, 6.0),
        "length": jax.random.randint(splits[2], (1,), TOKENS // 2, TOKENS + 1).astype(jnp.int32),
        "pair_gain": jnp.clip(1.0 + 0.15 * jax.random.normal(splits[3], (PAIR_DIM,), jnp.float32), 0.25, 1.75),
        "pair_proj": normal_values(splits[4], (4, PAIR_DIM, PAIR_DIM), PAIR_DIM ** -0.5, 0.375),
        "bias_weight": draw_bias_weight(jax.random.fold_in(splits[12], 71), 0),
        "pair_out_weight": normal_values(splits[6], (PAIR_DIM, PAIR_DIM), (PAIR_DIM // 8) ** -0.5, 1.0),
        "single_gain": jnp.clip(1.0 + 0.15 * jax.random.normal(splits[7], (SINGLE_DIM,), jnp.float32), 0.25, 1.75),
        "single_proj": normal_values(splits[8], (4, SINGLE_DIM, SINGLE_DIM), SINGLE_DIM ** -0.5, 0.21875, ((2, 8),)),
        "bias_norm_gain": jnp.clip(1.0 + 0.15 * jax.random.normal(splits[9], (PAIR_DIM,), jnp.float32), 0.25, 1.75),
        "single_bias_weight": draw_single_bias_weight(jax.random.fold_in(splits[12], 71), 0),
        "single_out_weight": normal_values(splits[11], (SINGLE_DIM, SINGLE_DIM), (SINGLE_DIM // 8) ** -0.5, 0.625, ((0, 8),)),
    }


masked_value = -1e+30

def normalize(values, scales):
    floated = values.astype(jnp.float32)
    center = lax.optimization_barrier(jnp.mean(floated, axis=-1, keepdims=True))
    spread = lax.optimization_barrier(jnp.mean(jnp.square(floated - center), axis=-1, keepdims=True))
    return ((floated - center) * lax.rsqrt(spread + 1e-05) * scales).astype(jnp.bfloat16)

def project(inputs, matrix):
    return jnp.dot(inputs, matrix, preferred_element_type=jnp.float32).astype(jnp.bfloat16)

def softmax_weights(scores):
    row_max = lax.optimization_barrier(jnp.max(scores, axis=-1, keepdims=True))
    exponent = jnp.exp(scores - row_max)
    return (exponent / lax.optimization_barrier(jnp.sum(exponent, axis=-1, keepdims=True))).astype(jnp.bfloat16)

def reference(pair_rep, single_rep, length, pair_gain, pair_proj, bias_weight, pair_out_weight, single_gain, single_proj, bias_norm_gain, single_bias_weight, single_out_weight):
    block_rows = math.gcd(TOKENS, 8)
    groups = TOKENS // block_rows
    stacked = pair_rep.reshape(groups, block_rows, TOKENS, PAIR_DIM)

    def triangle_bias(rows_block):
        normed = normalize(rows_block, pair_gain)
        return project(normed, bias_weight)
    tri_bias = lax.map(triangle_bias, stacked).reshape(TOKENS, TOKENS, PAIR_HEADS)
    tri_bias = jnp.transpose(tri_bias, (2, 0, 1)).astype(jnp.float32)
    usable = jnp.arange(TOKENS, dtype=jnp.int32) < length[0]
    pair_scale = 1.0 / math.sqrt(PAIR_HEAD_DIM)

    def attend(rows_block):
        normed = normalize(rows_block, pair_gain)
        shape_heads = (block_rows, TOKENS, PAIR_HEADS, PAIR_HEAD_DIM)
        queries = project(normed, pair_proj[0]).reshape(shape_heads).astype(jnp.float32)
        key_rows = project(normed, pair_proj[1]).reshape(shape_heads).astype(jnp.float32)
        value_rows = project(normed, pair_proj[2]).reshape(shape_heads).astype(jnp.float32)
        gating = jax.nn.sigmoid(jnp.dot(normed, pair_proj[3], preferred_element_type=jnp.float32))
        scores = jnp.einsum('ijhd,ikhd->ihjk', queries, key_rows) * pair_scale + tri_bias[None]
        scores = jnp.where(usable, scores, masked_value)
        weights = softmax_weights(scores)
        attended = jnp.einsum('ihjk,ikhd->ijhd', weights.astype(jnp.float32), value_rows)
        attended = attended.reshape(block_rows, TOKENS, PAIR_DIM)
        hidden = (gating * attended).astype(jnp.bfloat16)
        updated = (rows_block.astype(jnp.float32) + jnp.dot(hidden, pair_out_weight, preferred_element_type=jnp.float32)).astype(jnp.bfloat16)
        bias_normed = normalize(updated, bias_norm_gain)
        head_bias = project(bias_normed, single_bias_weight)
        return (updated, head_bias)
    pair_out, head_bias = lax.map(attend, stacked)
    pair_out = pair_out.reshape(TOKENS, TOKENS, PAIR_DIM)
    head_bias = jnp.transpose(head_bias.reshape(TOKENS, TOKENS, SINGLE_HEADS), (2, 0, 1)).astype(jnp.float32)
    single_normed = normalize(single_rep, single_gain)
    shape_single = (TOKENS, SINGLE_HEADS, SINGLE_HEAD_DIM)
    s_query = project(single_normed, single_proj[0]).reshape(shape_single).astype(jnp.float32)
    s_key = project(single_normed, single_proj[1]).reshape(shape_single).astype(jnp.float32)
    s_value = project(single_normed, single_proj[2]).reshape(shape_single).astype(jnp.float32)
    s_gate = jax.nn.sigmoid(jnp.dot(single_normed, single_proj[3], preferred_element_type=jnp.float32))
    scores = jnp.einsum('ihd,jhd->hij', s_query, s_key) / math.sqrt(SINGLE_HEAD_DIM) + head_bias
    scores = jnp.where(usable, scores, masked_value)
    weights = softmax_weights(scores)
    blended = jnp.einsum('hij,jhd->ihd', weights.astype(jnp.float32), s_value).reshape(TOKENS, SINGLE_DIM)
    s_hidden = (s_gate * blended).astype(jnp.bfloat16)
    single_out = (single_rep.astype(jnp.float32) + jnp.dot(s_hidden, single_out_weight, preferred_element_type=jnp.float32)).astype(jnp.bfloat16)
    return (pair_out, single_out)
```

```python
import functools
import math

import jax
import jax.numpy as jnp
from jax import lax
from jax.experimental import pallas as pl
from jax.experimental.pallas import tpu as pltpu
from jax.sharding import Mesh, PartitionSpec as P

F32 = jnp.float32
BF16 = jnp.bfloat16
TOKENS = 768
CHANNELS = 256
HEADS = 8
HEAD_DIM = 32
SINGLE_DIM = 768
SINGLE_HEADS = 16
SINGLE_HEAD_DIM = 48
ROWS = 48
COLS = 96
MINE = 6
LOG2E = 1.4426950408889634
MASKED = -1e30
ROW = ("x", "zl", "core")
COL = ("y", "zh")
VMEM_LIMIT = 56 * 2**20


def params():
    return pltpu.CompilerParams(vmem_limit_bytes=VMEM_LIMIT)


def whole(shape):
    zeros = (0,) * len(shape)
    return pl.BlockSpec(shape, lambda *_: zeros)


def normalize(values, scales):
    floated = values.astype(F32)
    center = jnp.mean(floated, axis=-1, keepdims=True)
    moved = floated - center
    spread = jnp.mean(jnp.square(moved), axis=-1, keepdims=True)
    return (moved * lax.rsqrt(spread + 1e-05) * scales).astype(BF16)


def dot(a, b):
    return jnp.dot(a, b, preferred_element_type=F32)


def dot_nt(a, b):
    return lax.dot_general(a, b, (((1,), (1,)), ((), ())), preferred_element_type=F32)


def local_bias_kernel(limit_ref, pair_ref, gain_ref, weight_ref, out_ref, held):
    limit = limit_ref[0]
    key = lax.broadcasted_iota(jnp.int32, (HEADS, COLS), 1)

    def step(block, carry):
        start = block * 8
        normed = normalize(pair_ref[pl.ds(start, 8)].reshape(8 * COLS, CHANNELS), gain_ref[...])
        bias = dot_nt(weight_ref[...], normed) * LOG2E
        for row in range(8):
            piece = jnp.where(key < limit, bias[:HEADS, row * COLS : (row + 1) * COLS], MASKED)
            held[:, pl.ds(start + row, 1), :] = piece[:, None, :]
        return carry

    lax.fori_loop(0, ROWS // 8, step, 0)
    out_ref[...] = held[...].astype(BF16)


def local_bias(limit, pair, gain, weight):
    return pl.pallas_call(
        local_bias_kernel,
        grid_spec=pltpu.PrefetchScalarGridSpec(
            num_scalar_prefetch=1,
            grid=(1,),
            in_specs=[
                whole((ROWS, COLS, CHANNELS)),
                whole((1, CHANNELS)),
                whole((16, CHANNELS)),
            ],
            out_specs=whole((HEADS, ROWS, COLS)),
            scratch_shapes=[pltpu.VMEM((HEADS, ROWS, COLS), F32)],
        ),
        out_shape=jax.ShapeDtypeStruct((HEADS, ROWS, COLS), BF16),
        compiler_params=params(),
    )(limit, pair, gain, weight)


def join_kernel(in_ref, out_ref):
    out_ref[0] = jnp.concatenate([in_ref[col, 0] for col in range(8)], axis=1)


def join(pieces):
    return pl.pallas_call(
        join_kernel,
        grid=(4, 2),
        in_specs=[pl.BlockSpec((8, 1, 2 * ROWS, COLS), lambda h, z: (z, h, 0, 0))],
        out_specs=pl.BlockSpec((1, 2 * ROWS, TOKENS), lambda h, z: (h, z, 0)),
        out_shape=jax.ShapeDtypeStruct((4, 4 * ROWS, TOKENS), BF16),
        compiler_params=params(),
    )(pieces)


def project_kernel(pair_ref, gain_ref, wq_ref, wkt_ref, wv_ref, wg_ref, q_ref, kt_ref, v_ref, g_ref):
    normed = normalize(pair_ref[:, 0].reshape(TOKENS, CHANNELS), gain_ref[...])
    q_ref[0] = (dot(normed, wq_ref[...]) * (LOG2E / math.sqrt(HEAD_DIM))).astype(BF16)
    kt_ref[0] = dot_nt(wkt_ref[...], normed).astype(BF16)
    v_ref[0] = dot(normed, wv_ref[...]).astype(BF16)
    g_ref[0] = jax.nn.sigmoid(dot(normed, wg_ref[...])).astype(BF16)


def project(pair, gain, wq, wkt, wv, wg):
    square = whole((CHANNELS, CHANNELS))
    token = pl.BlockSpec((1, TOKENS, CHANNELS), lambda i: (i, 0, 0))
    token_shape = jax.ShapeDtypeStruct((MINE, TOKENS, CHANNELS), BF16)
    return pl.pallas_call(
        project_kernel,
        grid=(MINE,),
        in_specs=[
            pl.BlockSpec((8, 1, COLS, CHANNELS), lambda i: (0, i, 0, 0)),
            whole((1, CHANNELS)),
            square,
            square,
            square,
            square,
        ],
        out_specs=[token, pl.BlockSpec((1, CHANNELS, TOKENS), lambda i: (i, 0, 0)), token, token],
        out_shape=[
            token_shape,
            jax.ShapeDtypeStruct((MINE, CHANNELS, TOKENS), BF16),
            token_shape,
            token_shape,
        ],
        compiler_params=params(),
    )(pair, gain, wq, wkt, wv, wg)


def attend_kernel(place_ref, q_ref, kt_ref, v_ref, g_ref, pair_ref, first_ref, second_ref, wo_ref, *rest):
    out_ref = rest[-1]
    span = 4 * ROWS
    q = q_ref[0]
    kt = kt_ref[0]
    v = v_ref[0]
    ones = jnp.ones((TOKENS, 128), BF16)
    lane = lax.broadcasted_iota(jnp.int32, (1, CHANNELS), 1)
    half_lane = lax.broadcasted_iota(jnp.int32, (1, 128), 1)
    halves = []
    for half, bias_ref in enumerate((first_ref, second_ref)):
        values = jnp.concatenate([v[:, 128 * half : 128 * half + 128], ones], axis=1)
        total = jnp.zeros((span, 128), F32)
        for head in range(4):
            low = HEAD_DIM * (4 * half + head)
            own = jnp.where((lane >= low) & (lane < low + HEAD_DIM), q, jnp.zeros_like(q))
            scores = dot(own, kt) + bias_ref[head].astype(F32)
            top = jnp.max(scores, axis=1, keepdims=True)
            weights = jnp.exp2(scores - top).astype(BF16)
            mixed = dot(weights, values)
            mixed = mixed[:, :128] / mixed[:, 128:]
            low = HEAD_DIM * head
            total = jnp.where((half_lane >= low) & (half_lane < low + HEAD_DIM), mixed, total)
        halves.append(total)
    attended = jnp.concatenate(halves, axis=1)
    hidden = (g_ref[0].astype(F32) * attended).astype(BF16)
    result = pair_ref[:, 0].reshape(span, CHANNELS).astype(F32) + dot(hidden, wo_ref[...])
    out_ref[:, 0] = result.astype(BF16).reshape(2, COLS, CHANNELS)


def attend(place, q, kt, v, g, pair, first, second, wo, buffer):
    span = 4 * ROWS
    part = pl.BlockSpec((1, span, CHANNELS), lambda i, place: (i, place[0], 0))
    block = pl.BlockSpec((2, 1, COLS, CHANNELS), lambda i, place: (place[0], i, 0, 0))
    specs = [
        part,
        pl.BlockSpec((1, CHANNELS, TOKENS), lambda i, place: (i, 0, 0)),
        pl.BlockSpec((1, TOKENS, CHANNELS), lambda i, place: (i, 0, 0)),
        part,
        block,
        whole((4, span, TOKENS)),
        whole((4, span, TOKENS)),
        whole((CHANNELS, CHANNELS)),
    ]
    operands = [q, kt, v, g, pair, first, second, wo]
    aliases = {}
    if buffer is not None:
        specs.append(pl.BlockSpec(memory_space=pl.ANY))
        operands.append(buffer)
        aliases = {len(operands): 0}
    return pl.pallas_call(
        attend_kernel,
        grid_spec=pltpu.PrefetchScalarGridSpec(
            num_scalar_prefetch=1,
            grid=(MINE,),
            in_specs=specs,
            out_specs=block,
        ),
        out_shape=jax.ShapeDtypeStruct((8, MINE, COLS, CHANNELS), BF16),
        input_output_aliases=aliases,
        compiler_params=params(),
    )(place, *operands)


def single_project_kernel(start_ref, single_ref, gain_ref, weight_ref, kv_ref, qg_ref):
    normed = normalize(single_ref[...], gain_ref[...])
    kv_ref[0] = dot_nt(weight_ref[0], normed).astype(BF16)
    kv_ref[1] = dot_nt(weight_ref[1], normed).astype(BF16)
    start = pl.multiple_of(start_ref[0], 16)
    own = normalize(single_ref[pl.ds(start, ROWS)], gain_ref[...])
    qg_ref[0] = dot_nt(own, weight_ref[2]) * (LOG2E / math.sqrt(SINGLE_HEAD_DIM))
    qg_ref[1] = jax.nn.sigmoid(dot_nt(own, weight_ref[3]))


def single_project(start, single, gain, weight):
    return pl.pallas_call(
        single_project_kernel,
        grid_spec=pltpu.PrefetchScalarGridSpec(
            num_scalar_prefetch=1,
            grid=(1,),
            in_specs=[
                whole((TOKENS, SINGLE_DIM)),
                whole((1, SINGLE_DIM)),
                whole((4, COLS, SINGLE_DIM)),
            ],
            out_specs=[whole((2, COLS, TOKENS)), whole((2, ROWS, COLS))],
        ),
        out_shape=[
            jax.ShapeDtypeStruct((2, COLS, TOKENS), BF16),
            jax.ShapeDtypeStruct((2, ROWS, COLS), F32),
        ],
        compiler_params=params(),
    )(start, single, gain, weight)


def single_kernel(limit_ref, pair_ref, gain_ref, weight_ref, q_ref, g_ref, kt_ref, v_ref, wo_ref, rep_ref, out_ref):
    heads = SINGLE_HEADS
    biases = []
    for i in range(MINE):
        normed = normalize(pair_ref[:, i].reshape(TOKENS, CHANNELS), gain_ref[...])
        biases.append(dot_nt(weight_ref[...], normed).astype(BF16).astype(F32))
    bias = jnp.concatenate(biases, axis=0) * LOG2E
    channel = lax.broadcasted_iota(jnp.int32, (heads, SINGLE_DIM), 1)
    low = lax.broadcasted_iota(jnp.int32, (heads, SINGLE_DIM), 0) * SINGLE_HEAD_DIM
    inside = (channel >= low) & (channel < low + SINGLE_HEAD_DIM)
    spread = [
        jnp.where(inside, jnp.broadcast_to(q_ref[i : i + 1], (heads, SINGLE_DIM)), 0.0)
        for i in range(MINE)
    ]
    scores = dot(jnp.concatenate(spread, axis=0).astype(BF16), kt_ref[...]) + bias
    key = lax.broadcasted_iota(jnp.int32, (1, TOKENS), 1)
    scores = jnp.where(key < limit_ref[0], scores, MASKED)
    top = jnp.max(scores, axis=1, keepdims=True)
    exponent = jnp.exp2(scores - top)
    total = jnp.sum(exponent, axis=1, keepdims=True)
    mixed = dot((exponent / total).astype(BF16), v_ref[...])
    rows = [
        jnp.sum(jnp.where(inside, mixed[heads * i : heads * (i + 1)], 0.0), axis=0, keepdims=True)
        for i in range(MINE)
    ]
    hidden = (g_ref[...] * jnp.concatenate(rows, axis=0)).astype(BF16)
    out_ref[...] = (rep_ref[...].astype(F32) + dot(hidden, wo_ref[...])).astype(BF16)


def single_attend(limit, pair, gain, weight, q, g, kt, v, wo, rep):
    rows = whole((MINE, SINGLE_DIM))
    square = whole((SINGLE_DIM, SINGLE_DIM))
    return pl.pallas_call(
        single_kernel,
        grid_spec=pltpu.PrefetchScalarGridSpec(
            num_scalar_prefetch=1,
            grid=(1,),
            in_specs=[
                whole((8, MINE, COLS, CHANNELS)),
                whole((1, CHANNELS)),
                whole((SINGLE_HEADS, CHANNELS)),
                rows,
                rows,
                square,
                square,
                square,
                rows,
            ],
            out_specs=rows,
        ),
        out_shape=jax.ShapeDtypeStruct((MINE, SINGLE_DIM), BF16),
        compiler_params=params(),
    )(limit, pair, gain, weight, q, g, kt, v, wo, rep)


def exchange(value):
    return lax.all_to_all(value, COL, split_axis=0, concat_axis=0, tiled=True)


def shift(value, axis, by):
    size = lax.axis_size(axis)
    return lax.ppermute(value, axis, [(i, (i + by) % size) for i in range(size)])


def per_device(
    pair_rep,
    single_rep,
    length,
    pair_gain,
    pair_proj,
    bias_weight,
    pair_out_weight,
    single_gain,
    single_proj,
    bias_norm_gain,
    single_bias_weight,
    single_out_weight,
):
    core = lax.axis_index("core")
    x = lax.axis_index("x")
    row = lax.axis_index(ROW)
    col = lax.axis_index(COL)
    second_core = core == 1
    pair_gain = pair_gain.reshape(1, CHANNELS)

    pair = exchange(pair_rep.reshape(8, MINE, COLS, CHANNELS))

    limit = length - col * COLS
    weight = jnp.concatenate([bias_weight.T, jnp.zeros((8, CHANNELS), BF16)], axis=0)
    bias = local_bias(limit, pair_rep, pair_gain, weight)
    low, high = bias[:4], bias[4:]
    kept = jnp.where(second_core, high, low)
    given = jnp.where(second_core, low, high)
    taken = shift(given, "core", 1)
    block = jnp.where(second_core, jnp.stack([taken, kept], 1), jnp.stack([kept, taken], 1))
    copies = jnp.broadcast_to(block.reshape(1, 4, 2 * ROWS, COLS), (16, 4, 2 * ROWS, COLS))
    pieces = lax.all_to_all(copies, ("zl", "y", "zh"), split_axis=0, concat_axis=0, tiled=True)
    own = join(pieces)
    firsts = [own, shift(own, "x", 1), shift(own, "x", -1), shift(own, "x", 2)]
    seconds = [shift(item, "core", 1) for item in firsts]
    places = [x, (x + 3) % 4, (x + 1) % 4, (x + 2) % 4]

    single_t = jnp.swapaxes(single_proj, 1, 2)
    single_t = jnp.stack([single_t[1], single_t[2], single_t[0], single_t[3]])
    kv, qg = single_project(
        (row * ROWS).reshape(1), single_rep, single_gain.reshape(1, SINGLE_DIM), single_t
    )
    shared = jnp.concatenate([kv, single_out_weight[None]], axis=0)
    gathered = lax.all_gather(shared, COL, axis=0, tiled=False)
    qg = jnp.swapaxes(qg.reshape(2, 8, MINE, COLS), 0, 1)
    qg = jnp.transpose(exchange(qg), (1, 2, 0, 3)).reshape(2, MINE, SINGLE_DIM)
    single_kt = gathered[:, 0].reshape(SINGLE_DIM, TOKENS)
    single_v = gathered[:, 1].reshape(SINGLE_DIM, TOKENS).T
    single_wo = gathered[:, 2].reshape(SINGLE_DIM, SINGLE_DIM)

    turned = jnp.where(second_core, jnp.roll(pair_proj, 128, axis=2), pair_proj)
    wo = jnp.where(second_core, jnp.roll(pair_out_weight, 128, axis=0), pair_out_weight)
    q, kt, v, g = project(pair, pair_gain, turned[0], turned[1].T, turned[2], turned[3])

    buffer = None
    for place, first, second in zip(places, firsts, seconds):
        buffer = attend(place.reshape(1), q, kt, v, g, pair, first, second, wo, buffer)
    pair_out = exchange(buffer).reshape(ROWS, COLS, CHANNELS)

    rep = lax.dynamic_slice_in_dim(single_rep, row * ROWS + col * MINE, MINE, 0)
    rows = single_attend(
        length,
        buffer,
        bias_norm_gain.reshape(1, CHANNELS),
        single_bias_weight.T,
        qg[0],
        qg[1],
        single_kt,
        single_v,
        single_wo,
        rep,
    )
    rows = jnp.swapaxes(rows.reshape(MINE, 8, COLS), 0, 1)
    single_out = exchange(rows).reshape(ROWS, COLS)
    return pair_out, single_out


def solution(mesh):
    fine = Mesh(mesh.devices.reshape(4, 2, 2, 4, 2), ROW + COL)
    in_specs = (
        P(ROW, COL, None),
        P(),
        P(),
        P(),
        P(),
        P(),
        P(),
        P(),
        P(None, None, COL),
        P(),
        P(),
        P(COL, None),
    )
    out_specs = (P(ROW, COL, None), P(ROW, COL))
    return jax.shard_map(
        per_device, mesh=fine, in_specs=in_specs, out_specs=out_specs, check_vma=False
    )
```

```python
import functools
import math

import jax
import jax.numpy as jnp
from jax import lax
from jax.experimental import pallas as pl
from jax.experimental.pallas import tpu as pltpu
from jax.sharding import Mesh, PartitionSpec as P

F32 = jnp.float32
BF16 = jnp.bfloat16
TOKENS = 768
CHANNELS = 256
HEADS = 8
HEAD_DIM = 32
SINGLE_DIM = 768
SINGLE_HEADS = 16
SINGLE_HEAD_DIM = 48
ROWS = 48
COLS = 96
MINE = 6
LOG2E = 1.4426950408889634
MASKED = -1e30
ROW = ("x", "zl", "core")
COL = ("y", "zh")
VMEM_LIMIT = 56 * 2**20


def params():
    return pltpu.CompilerParams(vmem_limit_bytes=VMEM_LIMIT)


def cost(time):
    return pl.CostEstimate(flops=time * 10000000, bytes_accessed=time * 30000, transcendentals=0)


def whole(shape):
    zeros = (0,) * len(shape)
    return pl.BlockSpec(shape, lambda *_: zeros)


def normalize(values, scales):
    floated = values.astype(F32)
    center = jnp.mean(floated, axis=-1, keepdims=True)
    moved = floated - center
    spread = jnp.mean(jnp.square(moved), axis=-1, keepdims=True)
    return (moved * lax.rsqrt(spread + 1e-05) * scales).astype(BF16)


def dot(a, b):
    return jnp.dot(a, b, preferred_element_type=F32)


def dot_nt(a, b):
    return lax.dot_general(a, b, (((1,), (1,)), ((), ())), preferred_element_type=F32)


def local_bias_kernel(limit_ref, pair_ref, gain_ref, weight_ref, out_ref, held):
    limit = limit_ref[0]
    key = lax.broadcasted_iota(jnp.int32, (HEADS, COLS), 1)
    weight = weight_ref[...]

    def step(block, carry):
        start = block * 8
        normed = normalize(pair_ref[pl.ds(start, 8)].reshape(8 * COLS, CHANNELS), gain_ref[...])
        bias = dot_nt(weight, normed) * LOG2E
        for row in range(8):
            piece = jnp.where(key < limit, bias[:, row * COLS : (row + 1) * COLS], MASKED)
            held[:, pl.ds(start + row, 1), :] = piece[:, None, :]
        return carry

    lax.fori_loop(0, ROWS // 8, step, 0)
    for half in range(2):
        out_ref[half] = jnp.concatenate([held[4 * half + h] for h in range(4)], axis=1).astype(BF16)


def local_bias(limit, pair, gain, weight):
    return pl.pallas_call(
        local_bias_kernel,
        grid_spec=pltpu.PrefetchScalarGridSpec(
            num_scalar_prefetch=1,
            grid=(1,),
            in_specs=[
                whole((ROWS, COLS, CHANNELS)),
                whole((1, CHANNELS)),
                whole((HEADS, CHANNELS)),
            ],
            out_specs=whole((2, ROWS, 4 * COLS)),
            scratch_shapes=[pltpu.VMEM((HEADS, ROWS, COLS), F32)],
        ),
        out_shape=jax.ShapeDtypeStruct((2, ROWS, 4 * COLS), BF16),
        compiler_params=params(),
        cost_estimate=cost(5),
    )(limit, pair, gain, weight)


def join_kernel(place_ref, a_ref, b_ref, c_ref, d_ref, o0_ref, o1_ref, held):
    y = place_ref[0]
    z = place_ref[1]
    for slot, ref in enumerate((a_ref, b_ref, c_ref, d_ref)):
        held[slot] = ref[...]
    for low in range(2):
        for core in range(2):
            blocks = []
            for col in range(8):
                depth = lax.rem(2 * (col % 2) + low - z + 4, 4)
                side = lax.rem(col // 2 - y + 4, 4)
                blocks.append(held[depth, side, core])
            for head in range(4):
                line = jnp.concatenate([b[:, COLS * head : COLS * (head + 1)] for b in blocks], axis=1)
                at = 2 * low + core
                o0_ref[head, 16 * at : 16 * (at + 1)] = line[32:]
                o1_ref[head, 32 * at : 32 * (at + 1)] = line[:32]


def join(place, pieces):
    shape = (4, 2, ROWS, 4 * COLS)
    outs = [(4, 4 * rows, TOKENS) for rows in (16, 32)]
    return pl.pallas_call(
        join_kernel,
        grid_spec=pltpu.PrefetchScalarGridSpec(
            num_scalar_prefetch=1,
            grid=(1,),
            in_specs=[whole(shape)] * 4,
            out_specs=[whole(out) for out in outs],
            scratch_shapes=[pltpu.VMEM((4,) + shape, BF16)],
        ),
        out_shape=[jax.ShapeDtypeStruct(out, BF16) for out in outs],
        compiler_params=params(),
        cost_estimate=cost(3),
    )(place, *pieces)


def project_kernel(pair_ref, gain_ref, wq_ref, wkt_ref, wv_ref, wg_ref, *rest):
    kt_ref, v_ref, q0_ref, q1_ref, g0_ref, g1_ref, old0_ref, old1_ref = rest[-8:]
    old = pair_ref[...].reshape(TOKENS, CHANNELS)
    normed = normalize(old, gain_ref[...])
    q = (dot(normed, wq_ref[...]) * (LOG2E / math.sqrt(HEAD_DIM))).astype(BF16)
    kt_ref[0] = dot_nt(wkt_ref[...], normed).astype(BF16)
    v_ref[0] = dot(normed, wv_ref[...]).astype(BF16)
    g = jax.nn.sigmoid(dot(normed, wg_ref[...])).astype(BF16)
    for value, ref0, ref1 in ((q, q0_ref, q1_ref), (g, g0_ref, g1_ref), (old, old0_ref, old1_ref)):
        value = value.reshape(16, ROWS, CHANNELS)
        ref0[0] = value[:, 32:].reshape(4, 64, CHANNELS)
        ref1[0] = value[:, :32].reshape(4, 128, CHANNELS)


def project(pair, gain, wq, wkt, wv, wg, start, buffers):
    square = whole((CHANNELS, CHANNELS))
    blocks = [(CHANNELS, TOKENS), (TOKENS, CHANNELS)] + [(4, 64, CHANNELS), (4, 128, CHANNELS)] * 3
    operands = [pair, gain, wq, wkt, wv, wg]
    aliases = {len(operands) + n: n for n in range(len(buffers))}

    def spec(block):
        zeros = (0,) * len(block)
        return pl.BlockSpec((1,) + block, lambda i: (start + i,) + zeros)

    return pl.pallas_call(
        project_kernel,
        grid=(MINE // 2,),
        in_specs=[
            pl.BlockSpec((8, 6, 16, CHANNELS), lambda i: (0, i, 0, 0)),
            whole((1, CHANNELS)),
            square,
            square,
            square,
            square,
        ]
        + [pl.BlockSpec(memory_space=pl.ANY)] * len(buffers),
        out_specs=[spec(block) for block in blocks],
        out_shape=[jax.ShapeDtypeStruct((MINE,) + block, BF16) for block in blocks],
        input_output_aliases=aliases,
        compiler_params=params(),
        cost_estimate=cost(5),
    )(*operands, *buffers)


def attend_chunk(order, span, q_ref, g_ref, old_ref, firsts, seconds, kt, v, wo):
    q = jnp.concatenate([q_ref[0, at] for at in order], axis=0)
    ones = jnp.ones((TOKENS, 128), BF16)
    lane = lax.broadcasted_iota(jnp.int32, (1, CHANNELS), 1)
    half_lane = lax.broadcasted_iota(jnp.int32, (1, 128), 1)
    halves = []
    for half, refs in enumerate((firsts, seconds)):
        values = jnp.concatenate([v[:, 128 * half : 128 * half + 128], ones], axis=1)
        total = jnp.zeros((4 * span, 128), F32)
        for head in range(4):
            low = HEAD_DIM * (4 * half + head)
            own = jnp.where((lane >= low) & (lane < low + HEAD_DIM), q, jnp.zeros_like(q))
            bias = jnp.concatenate([ref[head] for ref in refs], axis=0)
            scores = dot(own, kt) + bias.astype(F32)
            top = jnp.max(scores, axis=1, keepdims=True)
            weights = jnp.exp2(scores - top).astype(BF16)
            mixed = dot(weights, values)
            mixed = mixed[:, :128] / mixed[:, 128:]
            low = HEAD_DIM * head
            total = jnp.where((half_lane >= low) & (half_lane < low + HEAD_DIM), mixed, total)
        halves.append(total)
    attended = jnp.concatenate(halves, axis=1)
    g = jnp.concatenate([g_ref[0, at] for at in order], axis=0)
    update = dot((g.astype(F32) * attended).astype(BF16), wo)
    return [
        (old_ref[0, at].astype(F32) + update[span * step : span * (step + 1)]).astype(BF16)
        for step, at in enumerate(order)
    ]


def attend_kernel(x_ref, kt_ref, v_ref, wo_ref, q_ref, g_ref, old_ref, *rest):
    out_ref = rest[-1]
    order = [lax.rem(x_ref[0] + step, 4) for step in range(4)]
    span = q_ref.shape[2]
    parts = attend_chunk(
        order, span, q_ref, g_ref, old_ref, rest[:4], rest[4:8], kt_ref[0], v_ref[0], wo_ref[...]
    )
    for at, part in zip(order, parts):
        out_ref[pl.ds(2 * at, 2), 0] = part.reshape(2, 2, span // 4, CHANNELS)


def attend_late_kernel(x_ref, kt_ref, v_ref, wo_ref, q0_ref, g0_ref, old0_ref, q1_ref, g1_ref, old1_ref, *rest):
    out_ref = rest[-1]
    order = [lax.rem(x_ref[0] + step, 4) for step in range(4)]
    chunks = ((q0_ref, g0_ref, old0_ref, rest[:8]), (q1_ref, g1_ref, old1_ref, rest[8:16]))
    for chunk, (q_ref, g_ref, old_ref, bias) in enumerate(chunks):
        span = q_ref.shape[2]
        parts = attend_chunk(
            order, span, q_ref, g_ref, old_ref, bias[:4], bias[4:], kt_ref[0], v_ref[0], wo_ref[...]
        )
        count = chunk + 1
        for at, part in zip(order, parts):
            part = part.reshape(2, 2, count, 16, CHANNELS)
            for core in range(2):
                first = 3 * core + (2 if chunk == 0 else 0)
                out_ref[pl.ds(2 * at, 2), first : first + count] = part[:, core]


def attend(x, kt, v, wo, chunks, rows, start, out_block, out_index, out_shape, buffer, time):
    def spec(shape):
        zeros = (0,) * len(shape)
        return pl.BlockSpec((1,) + shape, lambda i, x: (start + i,) + zeros)

    operands = [x, kt, v, wo]
    specs = [spec((CHANNELS, TOKENS)), spec((TOKENS, CHANNELS)), whole((CHANNELS, CHANNELS))]
    for tokens, _ in chunks:
        operands += tokens
        specs += [spec(token.shape[1:]) for token in tokens]
    for _, biases in chunks:
        operands += biases
        specs += [whole(bias.shape) for bias in biases]
    aliases = {}
    if buffer is not None:
        aliases = {len(operands): 0}
        specs.append(pl.BlockSpec(memory_space=pl.ANY))
        operands.append(buffer)
    return pl.pallas_call(
        attend_kernel if len(chunks) == 1 else attend_late_kernel,
        grid_spec=pltpu.PrefetchScalarGridSpec(
            num_scalar_prefetch=1,
            grid=(rows,),
            in_specs=specs,
            out_specs=pl.BlockSpec(out_block, out_index),
        ),
        out_shape=jax.ShapeDtypeStruct(out_shape, BF16),
        input_output_aliases=aliases,
        compiler_params=params(),
        cost_estimate=cost(time * 100),
    )(*operands)


def single_project_kernel(place_ref, single_ref, gain_ref, weight_ref, kv_ref, qg_ref):
    normed = normalize(single_ref[...], gain_ref[...])
    for kind in range(2):
        both = dot_nt(weight_ref[1 + kind], normed).astype(BF16)
        for head in range(2):
            kv_ref[head, kind] = both[SINGLE_HEAD_DIM * head : SINGLE_HEAD_DIM * (head + 1)]
    start = pl.multiple_of(place_ref[0], 16)
    own = normalize(single_ref[pl.ds(start, ROWS)], gain_ref[...])
    q = dot_nt(own, weight_ref[0]) * (LOG2E / math.sqrt(SINGLE_HEAD_DIM))
    g = jax.nn.sigmoid(dot_nt(own, weight_ref[3]))
    for kind, value in enumerate((q, g)):
        turned = jnp.concatenate([value[:, SINGLE_HEAD_DIM:], value[:, :SINGLE_HEAD_DIM]], axis=1)
        qg_ref[kind] = jnp.where(place_ref[1] == 1, turned, value)


def single_project(place, single, gain, weight):
    return pl.pallas_call(
        single_project_kernel,
        grid_spec=pltpu.PrefetchScalarGridSpec(
            num_scalar_prefetch=1,
            grid=(1,),
            in_specs=[
                whole((TOKENS, SINGLE_DIM)),
                whole((1, SINGLE_DIM)),
                whole((4, COLS, SINGLE_DIM)),
            ],
            out_specs=[whole((2, 2, SINGLE_HEAD_DIM, TOKENS)), whole((2, ROWS, COLS))],
        ),
        out_shape=[
            jax.ShapeDtypeStruct((2, 2, SINGLE_HEAD_DIM, TOKENS), BF16),
            jax.ShapeDtypeStruct((2, ROWS, COLS), F32),
        ],
        compiler_params=params(),
        cost_estimate=cost(4),
    )(place, single, gain, weight)


def single_kernel(
    place_ref, early_ref, late_ref, gain_ref, weight_ref, extra_ref, *rest
):
    heads = SINGLE_HEADS
    shared, rep_ref, out_ref, held = rest[:8], rest[8], rest[9], rest[10]
    for core in range(2):
        for slot in range(4):
            held[core, lax.rem(place_ref[1] + slot, 4)] = shared[4 * core + slot][...]
    weight = weight_ref[...].astype(F32)
    line = lax.broadcasted_iota(jnp.int32, weight.shape, 0)
    turned = jnp.where(line % 2 == 0, pltpu.roll(weight, heads - 1, 0), pltpu.roll(weight, 1, 0))
    weight = jnp.where(place_ref[2] == 1, turned, weight).astype(BF16)
    biases = []
    for i in range(MINE):
        tokens = early_ref[:, i] if i < 4 else late_ref[:, 6 * (i - 4) : 6 * (i - 3)]
        normed = normalize(tokens.reshape(TOKENS, CHANNELS), gain_ref[...])
        biases.append(dot_nt(weight, normed).astype(BF16).astype(F32))
    bias = jnp.concatenate(biases, axis=0) * LOG2E

    def piece(core, col, kind, band, third):
        at = 9 * kind + 3 * band + third
        return held[core, at // 7, col, at % 7]

    def matrix(kind):
        rows = []
        for col in range(8):
            for core in range(2):
                for band in range(3):
                    rows.append(
                        jnp.concatenate([piece(core, col, kind, band, third) for third in range(3)], axis=1)
                    )
        return jnp.concatenate(rows, axis=0)

    def vectors(low):
        return jnp.concatenate(
            [extra_ref[col, 0, low : low + MINE, :COLS].astype(F32) for col in range(8)], axis=1
        )

    q = vectors(0)
    g = vectors(8)
    channel = lax.broadcasted_iota(jnp.int32, (heads, SINGLE_DIM), 1)
    low = lax.broadcasted_iota(jnp.int32, (heads, SINGLE_DIM), 0) * SINGLE_HEAD_DIM
    inside = (channel >= low) & (channel < low + SINGLE_HEAD_DIM)
    spread = [
        jnp.where(inside, jnp.broadcast_to(q[i : i + 1], (heads, SINGLE_DIM)), 0.0)
        for i in range(MINE)
    ]
    scores = dot(jnp.concatenate(spread, axis=0).astype(BF16), matrix(0)) + bias
    key = lax.broadcasted_iota(jnp.int32, (1, TOKENS), 1)
    scores = jnp.where(key < place_ref[0], scores, MASKED)
    top = jnp.max(scores, axis=1, keepdims=True)
    exponent = jnp.exp2(scores - top)
    total = jnp.sum(exponent, axis=1, keepdims=True)
    mixed = dot_nt((exponent / total).astype(BF16), matrix(1))
    rows = [
        jnp.sum(jnp.where(inside, mixed[heads * i : heads * (i + 1)], 0.0), axis=0, keepdims=True)
        for i in range(MINE)
    ]
    hidden = (g * jnp.concatenate(rows, axis=0)).astype(BF16)
    result = rep_ref[...].astype(F32) + dot(hidden, matrix(2))
    result = jnp.concatenate([result, jnp.zeros((16 - MINE, SINGLE_DIM), F32)], axis=0)
    out_ref[...] = jnp.zeros(out_ref.shape, BF16)
    for col in range(8):
        out_ref[col, 0, :, :COLS] = result[:, COLS * col : COLS * (col + 1)].astype(BF16)


def single_attend(place, early, late, gain, weight, pair, shared, rep):
    shape = (8, 7, 16, CHANNELS)
    last = lambda *_: (0, 3 * MINE, 0, 0)
    return pl.pallas_call(
        single_kernel,
        grid_spec=pltpu.PrefetchScalarGridSpec(
            num_scalar_prefetch=1,
            grid=(1,),
            in_specs=[
                whole((8, 4, 2, ROWS, CHANNELS)),
                whole((8, 2 * MINE + 1, 16, CHANNELS)),
                whole((1, CHANNELS)),
                whole((SINGLE_HEADS, CHANNELS)),
                pl.BlockSpec((8, 1, 16, CHANNELS), last),
            ]
            + [whole(shape)] * 8
            + [whole((MINE, SINGLE_DIM))],
            scratch_shapes=[pltpu.VMEM((2, 4) + shape, BF16)],
            out_specs=pl.BlockSpec((8, 1, 16, CHANNELS), lambda *_: (0, 2 * MINE, 0, 0)),
        ),
        out_shape=jax.ShapeDtypeStruct((8, 2 * MINE + 1, 16, CHANNELS), BF16),
        input_output_aliases={2: 0},
        compiler_params=params(),
        cost_estimate=cost(700),
    )(place, early, late, gain, weight, pair, *shared, rep)


def exchange(value):
    return lax.all_to_all(value, COL, split_axis=0, concat_axis=0, tiled=True)


Z = ("zl", "zh")


def shift(value, axis, by):
    if axis == Z:
        ring = [0, 2, 1, 3]
        pairs = [(ring[i], ring[(i + by) % 4]) for i in range(4)]
    else:
        size = lax.axis_size(axis)
        pairs = [(i, (i + by) % size) for i in range(size)]
    return lax.ppermute(value, axis, pairs)


def around(value, axis):
    return [value, shift(value, axis, -1), shift(value, axis, 2), shift(value, axis, 1)]


def per_device(
    pair_rep,
    single_rep,
    length,
    pair_gain,
    pair_proj,
    bias_weight,
    pair_out_weight,
    single_gain,
    single_proj,
    bias_norm_gain,
    single_bias_weight,
    single_out_weight,
):
    core = lax.axis_index("core")
    x = lax.axis_index("x")
    row = lax.axis_index(ROW)
    col = lax.axis_index(COL)
    second_core = core == 1
    pair_gain = pair_gain.reshape(1, CHANNELS)

    groups = pair_rep.reshape(8, 6 * MINE, 16, CHANNELS)
    limit = length - col * COLS
    bias = local_bias(limit, pair_rep, pair_gain, bias_weight.T)
    kept = lax.dynamic_index_in_dim(bias, core, 0, False)
    given = lax.dynamic_index_in_dim(bias, 1 - core, 0, False)
    taken = shift(given, "core", 1)
    block = jnp.where(second_core, jnp.stack([taken, kept]), jnp.stack([kept, taken]))
    sides = jnp.stack(around(block, "y"))
    after, sides = lax.optimization_barrier((single_rep, sides))
    kv, qg = single_project(
        jnp.stack([row * ROWS, core]),
        after,
        single_gain.reshape(1, SINGLE_DIM),
        jnp.swapaxes(single_proj, 1, 2),
    )
    pieces = around(sides, Z)
    extra = qg.astype(BF16).reshape(2, 8, MINE, COLS)
    extra = jnp.pad(jnp.swapaxes(extra, 0, 1), ((0, 0), (0, 0), (0, 2), (0, CHANNELS - COLS)))
    shared = jnp.concatenate(
        [
            lax.dynamic_index_in_dim(kv, core, 0, False),
            lax.dynamic_slice_in_dim(single_out_weight, core * SINGLE_HEAD_DIM, SINGLE_HEAD_DIM, 0)[None],
        ],
        axis=0,
    )
    shared = jnp.transpose(shared.reshape(3, 3, 16, 3, CHANNELS), (0, 1, 3, 2, 4)).reshape(27, 16, CHANNELS)
    shared = jnp.pad(shared, ((0, 1), (0, 0), (0, 0)))
    shared = lax.dynamic_slice_in_dim(shared, 7 * x, 7, 0)
    message = jnp.concatenate(
        [
            groups[:, 3 * MINE :],
            extra.reshape(8, 1, 16, CHANNELS),
            jnp.broadcast_to(shared[None], (8, 7, 16, CHANNELS)),
        ],
        axis=1,
    )
    near, pieces = lax.optimization_barrier((groups[:, : 3 * MINE], pieces))
    near = exchange(near)
    message, near = lax.optimization_barrier((message, near))
    far = exchange(message)

    turned = jnp.where(second_core, jnp.roll(pair_proj, 128, axis=2), pair_proj)
    wo = jnp.where(second_core, jnp.roll(pair_out_weight, 128, axis=0), pair_out_weight)
    weights = (pair_gain, turned[0], turned[1].T, turned[2], turned[3])
    held = project(near, *weights, 0, ())

    depth = 2 * lax.axis_index("zh") + lax.axis_index("zl")
    chunks = join(jnp.stack([lax.axis_index("y"), depth]), pieces)
    firsts = [around(chunks[0], "x")]
    chunk, firsts[0][1] = lax.optimization_barrier((chunks[1], firsts[0][1]))
    firsts.append(around(chunk, "x"))
    seconds = [[shift(item, "core", 1) for item in items] for items in firsts]
    shared = far[:, 3 * MINE + 1 :]
    shared, _ = lax.optimization_barrier((shared, firsts[1][1]))
    shared = around(shared, "x")
    swapped = [shift(item, "core", 1) for item in shared]

    held = project(far, *weights, MINE // 2, held)
    kt, v = held[:2]
    tokens = [list(held[2 + chunk :: 2]) for chunk in range(2)]
    biases = [firsts[chunk] + seconds[chunk] for chunk in range(2)]
    parts = [(tokens[chunk], biases[chunk]) for chunk in range(2)]
    x1 = x.reshape(1)
    shape = (8, 4, 2, ROWS, CHANNELS)
    early = attend(
        x1, kt, v, wo, parts[:1], 4, 0, (8, 1, 2, 16, CHANNELS), lambda i, x: (0, i, 0, 2, 0), shape, None, 12
    )
    early = attend(
        x1, kt, v, wo, parts[1:], 4, 0, (8, 1, 2, 32, CHANNELS), lambda i, x: (0, i, 0, 0, 0), shape, early, 22
    )
    early, _ = lax.optimization_barrier((early, shared))
    late = attend(
        x1, kt, v, wo, parts, 2, 4, (8, 6, 16, CHANNELS), lambda i, x: (0, i, 0, 0), (8, 13, 16, CHANNELS), None, 16
    )
    rep = lax.dynamic_slice_in_dim(single_rep, row * ROWS + col * MINE, MINE, 0)
    late = single_attend(
        jnp.concatenate([length, x1, core.reshape(1)]),
        early,
        late,
        bias_norm_gain.reshape(1, CHANNELS),
        single_bias_weight.T,
        far,
        shared + swapped,
        rep,
    )
    early = exchange(early)
    early, late = lax.optimization_barrier((early, late))
    late = exchange(late)
    single_out = late[:, 2 * MINE, :MINE, :COLS].reshape(ROWS, COLS)
    parts = [early.reshape(8, 4, COLS, CHANNELS), late[:, : 2 * MINE].reshape(8, 2, COLS, CHANNELS)]
    return jnp.concatenate(parts, axis=1).reshape(ROWS, COLS, CHANNELS), single_out


def solution(mesh):
    fine = Mesh(mesh.devices.reshape(4, 2, 2, 4, 2), ROW + COL)
    in_specs = (
        P(ROW, COL, None),
        P(),
        P(),
        P(),
        P(),
        P(),
        P(),
        P(),
        P(None, None, COL),
        P(),
        P(),
        P(COL, None),
    )
    out_specs = (P(ROW, COL, None), P(ROW, COL))
    return jax.shard_map(
        per_device, mesh=fine, in_specs=in_specs, out_specs=out_specs, check_vma=False
    )
```

```python
import functools
import math

import jax
import jax.numpy as jnp
from jax import lax
from jax.experimental import pallas as pl
from jax.experimental.pallas import tpu as pltpu
from jax.sharding import Mesh, PartitionSpec as P

F32 = jnp.float32
BF16 = jnp.bfloat16
TOKENS = 768
CHANNELS = 256
HEADS = 8
HEAD_DIM = 32
SINGLE_DIM = 768
SINGLE_HEADS = 16
SINGLE_HEAD_DIM = 48
ROWS = 48
COLS = 96
MINE = 6
LOG2E = 1.4426950408889634
MASKED = -1e30
ROW = ("x", "zl", "core")
COL = ("y", "zh")
VMEM_LIMIT = 56 * 2**20


def params():
    return pltpu.CompilerParams(vmem_limit_bytes=VMEM_LIMIT)


def cost(time):
    return pl.CostEstimate(flops=time * 10000000, bytes_accessed=time * 30000, transcendentals=0)


def whole(shape):
    zeros = (0,) * len(shape)
    return pl.BlockSpec(shape, lambda *_: zeros)


def normalize(values, scales):
    floated = values.astype(F32)
    center = jnp.mean(floated, axis=-1, keepdims=True)
    moved = floated - center
    spread = jnp.mean(jnp.square(moved), axis=-1, keepdims=True)
    return (moved * lax.rsqrt(spread + 1e-05) * scales).astype(BF16)


def dot(a, b):
    return jnp.dot(a, b, preferred_element_type=F32)


def dot_nt(a, b):
    return lax.dot_general(a, b, (((1,), (1,)), ((), ())), preferred_element_type=F32)


def local_bias_kernel(limit_ref, pair_ref, gain_ref, weight_ref, out_ref, held):
    limit = limit_ref[0]
    key = lax.broadcasted_iota(jnp.int32, (HEADS, COLS), 1)
    weight = weight_ref[...]

    def step(block, carry):
        start = block * 8
        normed = normalize(pair_ref[pl.ds(start, 8)].reshape(8 * COLS, CHANNELS), gain_ref[...])
        bias = dot_nt(weight, normed) * LOG2E
        for row in range(8):
            piece = jnp.where(key < limit, bias[:, row * COLS : (row + 1) * COLS], MASKED)
            held[:, pl.ds(start + row, 1), :] = piece[:, None, :]
        return carry

    lax.fori_loop(0, ROWS // 8, step, 0)
    for half in range(2):
        out_ref[half] = jnp.concatenate([held[4 * half + h] for h in range(4)], axis=1).astype(BF16)


def local_bias(limit, pair, gain, weight):
    return pl.pallas_call(
        local_bias_kernel,
        grid_spec=pltpu.PrefetchScalarGridSpec(
            num_scalar_prefetch=1,
            grid=(1,),
            in_specs=[
                whole((ROWS, COLS, CHANNELS)),
                whole((1, CHANNELS)),
                whole((HEADS, CHANNELS)),
            ],
            out_specs=whole((2, ROWS, 4 * COLS)),
            scratch_shapes=[pltpu.VMEM((HEADS, ROWS, COLS), F32)],
        ),
        out_shape=jax.ShapeDtypeStruct((2, ROWS, 4 * COLS), BF16),
        compiler_params=params(),
        cost_estimate=cost(5),
    )(limit, pair, gain, weight)


def join_kernel(place_ref, a_ref, b_ref, c_ref, d_ref, out_ref, held):
    y = place_ref[0]
    z = place_ref[1]
    for slot, ref in enumerate((a_ref, b_ref, c_ref, d_ref)):
        held[slot] = ref[...]
    for low in range(2):
        for core in range(2):
            blocks = []
            for col in range(8):
                depth = lax.rem(2 * (col % 2) + low - z + 4, 4)
                side = lax.rem(col // 2 - y + 4, 4)
                blocks.append(held[depth, side, core])
            for head in range(4):
                line = jnp.concatenate([b[:, COLS * head : COLS * (head + 1)] for b in blocks], axis=1)
                at = ROWS * (2 * low + core)
                out_ref[head, at : at + ROWS] = line


def join(place, pieces):
    shape = (4, 2, ROWS, 4 * COLS)
    out = (4, 4 * ROWS, TOKENS)
    return pl.pallas_call(
        join_kernel,
        grid_spec=pltpu.PrefetchScalarGridSpec(
            num_scalar_prefetch=1,
            grid=(1,),
            in_specs=[whole(shape)] * 4,
            out_specs=whole(out),
            scratch_shapes=[pltpu.VMEM((4,) + shape, BF16)],
        ),
        out_shape=jax.ShapeDtypeStruct(out, BF16),
        compiler_params=params(),
        cost_estimate=cost(3),
    )(place, *pieces)


def project_kernel(pair_ref, gain_ref, wq_ref, wkt_ref, wv_ref, wg_ref, kt_ref, v_ref, q_ref, g_ref):
    normed = normalize(pair_ref[...].reshape(TOKENS, CHANNELS), gain_ref[...])
    q = (dot(normed, wq_ref[...]) * (LOG2E / math.sqrt(HEAD_DIM))).astype(BF16)
    kt_ref[0] = dot_nt(wkt_ref[...], normed).astype(BF16)
    v_ref[0] = dot(normed, wv_ref[...]).astype(BF16)
    g = jax.nn.sigmoid(dot(normed, wg_ref[...])).astype(BF16)
    q_ref[0] = q.reshape(4, 4 * ROWS, CHANNELS)
    g_ref[0] = g.reshape(4, 4 * ROWS, CHANNELS)


def project(pair, gain, wq, wkt, wv, wg):
    square = whole((CHANNELS, CHANNELS))
    blocks = [(CHANNELS, TOKENS), (TOKENS, CHANNELS)] + [(4, 4 * ROWS, CHANNELS)] * 2

    def spec(block):
        zeros = (0,) * len(block)
        return pl.BlockSpec((1,) + block, lambda i: (i,) + zeros)

    return pl.pallas_call(
        project_kernel,
        grid=(MINE,),
        in_specs=[
            pl.BlockSpec((8, 6, 16, CHANNELS), lambda i: (0, i, 0, 0)),
            whole((1, CHANNELS)),
            square,
            square,
            square,
            square,
        ],
        out_specs=[spec(block) for block in blocks],
        out_shape=[jax.ShapeDtypeStruct((MINE,) + block, BF16) for block in blocks],
        compiler_params=params(),
        cost_estimate=cost(5),
    )(pair, gain, wq, wkt, wv, wg)


def attend_kernel(x_ref, kt_ref, v_ref, q_ref, g_ref, pair_ref, wo_ref, *rest):
    firsts, seconds, out_ref = rest[:5], rest[5:10], rest[10]
    order = [lax.rem(x_ref[0] + step, 4) for step in range(4)]
    span = 4 * ROWS
    kt = kt_ref[0]
    v = v_ref[0]
    q = jnp.concatenate([q_ref[0, at] for at in order], axis=0)
    ones = jnp.ones((TOKENS, 128), BF16)
    lane = lax.broadcasted_iota(jnp.int32, (1, CHANNELS), 1)
    half_lane = lax.broadcasted_iota(jnp.int32, (1, 128), 1)
    halves = []
    for half, refs in enumerate((firsts, seconds)):
        values = jnp.concatenate([v[:, 128 * half : 128 * half + 128], ones], axis=1)
        total = jnp.zeros((TOKENS, 128), F32)
        for head in range(4):
            low = HEAD_DIM * (4 * half + head)
            own = jnp.where((lane >= low) & (lane < low + HEAD_DIM), q, jnp.zeros_like(q))
            low_heads, high_heads = refs[2], refs[3]
            far = low_heads[head] if head < 2 else high_heads[head - 2]
            bias = jnp.concatenate([refs[0][head], refs[1][head], far, refs[4][head]], axis=0)
            scores = dot(own, kt) + bias.astype(F32)
            top = jnp.max(scores, axis=1, keepdims=True)
            weights = jnp.exp2(scores - top).astype(BF16)
            mixed = dot(weights, values)
            mixed = mixed[:, :128] / mixed[:, 128:]
            low = HEAD_DIM * head
            total = jnp.where((half_lane >= low) & (half_lane < low + HEAD_DIM), mixed, total)
        halves.append(total)
    attended = jnp.concatenate(halves, axis=1)
    g = jnp.concatenate([g_ref[0, at] for at in order], axis=0)
    update = dot((g.astype(F32) * attended).astype(BF16), wo_ref[...])
    for step, at in enumerate(order):
        old = pair_ref[pl.ds(2 * at, 2)].reshape(span, CHANNELS).astype(F32)
        new = (old + update[span * step : span * (step + 1)]).astype(BF16)
        out_ref[pl.ds(2 * at, 2)] = new.reshape(2, 6, 16, CHANNELS)


def attend(x, kt, v, q, g, pair, wo, biases, rows, start, groups, time):
    def spec(shape):
        zeros = (0,) * len(shape)
        return pl.BlockSpec((1,) + shape, lambda i, x: (start + i,) + zeros)

    parts = spec((4, 4 * ROWS, CHANNELS))
    return pl.pallas_call(
        attend_kernel,
        grid_spec=pltpu.PrefetchScalarGridSpec(
            num_scalar_prefetch=1,
            grid=(rows,),
            in_specs=[
                spec((CHANNELS, TOKENS)),
                spec((TOKENS, CHANNELS)),
                parts,
                parts,
                pl.BlockSpec((8, 6, 16, CHANNELS), lambda i, x: (0, start + i, 0, 0)),
                whole((CHANNELS, CHANNELS)),
            ]
            + [whole(bias.shape) for bias in biases],
            out_specs=pl.BlockSpec((8, 6, 16, CHANNELS), lambda i, x: (0, i, 0, 0)),
        ),
        out_shape=jax.ShapeDtypeStruct((8, groups, 16, CHANNELS), BF16),
        compiler_params=params(),
        cost_estimate=cost(time * 100),
    )(x, kt, v, q, g, pair, wo, *biases)


def single_project_kernel(place_ref, single_ref, gain_ref, weight_ref, kv_ref, qg_ref):
    normed = normalize(single_ref[...], gain_ref[...])
    for kind in range(2):
        both = dot_nt(weight_ref[1 + kind], normed).astype(BF16)
        for head in range(2):
            kv_ref[head, kind] = both[SINGLE_HEAD_DIM * head : SINGLE_HEAD_DIM * (head + 1)]
    start = pl.multiple_of(place_ref[0], 16)
    own = normalize(single_ref[pl.ds(start, ROWS)], gain_ref[...])
    q = dot_nt(own, weight_ref[0]) * (LOG2E / math.sqrt(SINGLE_HEAD_DIM))
    g = jax.nn.sigmoid(dot_nt(own, weight_ref[3]))
    for kind, value in enumerate((q, g)):
        turned = jnp.concatenate([value[:, SINGLE_HEAD_DIM:], value[:, :SINGLE_HEAD_DIM]], axis=1)
        qg_ref[kind] = jnp.where(place_ref[1] == 1, turned, value)


def single_project(place, single, gain, weight):
    return pl.pallas_call(
        single_project_kernel,
        grid_spec=pltpu.PrefetchScalarGridSpec(
            num_scalar_prefetch=1,
            grid=(1,),
            in_specs=[
                whole((TOKENS, SINGLE_DIM)),
                whole((1, SINGLE_DIM)),
                whole((4, COLS, SINGLE_DIM)),
            ],
            out_specs=[whole((2, 2, SINGLE_HEAD_DIM, TOKENS)), whole((2, ROWS, COLS))],
        ),
        out_shape=[
            jax.ShapeDtypeStruct((2, 2, SINGLE_HEAD_DIM, TOKENS), BF16),
            jax.ShapeDtypeStruct((2, ROWS, COLS), F32),
        ],
        compiler_params=params(),
        cost_estimate=cost(4),
    )(place, single, gain, weight)


def single_kernel(
    place_ref, early_ref, late_ref, gain_ref, weight_ref, extra_ref, *rest
):
    heads = SINGLE_HEADS
    shared, rep_ref, out_ref, held = rest[:8], rest[8], rest[9], rest[10]
    for core in range(2):
        for slot in range(4):
            held[core, lax.rem(place_ref[1] + slot, 4)] = shared[4 * core + slot][...]
    weight = weight_ref[...].astype(F32)
    line = lax.broadcasted_iota(jnp.int32, weight.shape, 0)
    turned = jnp.where(line % 2 == 0, pltpu.roll(weight, heads - 1, 0), pltpu.roll(weight, 1, 0))
    weight = jnp.where(place_ref[2] == 1, turned, weight).astype(BF16)
    biases = []
    for i in range(MINE):
        tokens = early_ref[:, 6 * i : 6 * i + 6] if i < 4 else late_ref[:, 6 * i - 24 : 6 * i - 18]
        normed = normalize(tokens.reshape(TOKENS, CHANNELS), gain_ref[...])
        biases.append(dot_nt(weight, normed).astype(BF16).astype(F32))
    bias = jnp.concatenate(biases, axis=0) * LOG2E

    def piece(core, col, kind, band, third):
        at = 9 * kind + 3 * band + third
        return held[core, at // 7, col, at % 7]

    def matrix(kind):
        rows = []
        for col in range(8):
            for core in range(2):
                for band in range(3):
                    rows.append(
                        jnp.concatenate([piece(core, col, kind, band, third) for third in range(3)], axis=1)
                    )
        return jnp.concatenate(rows, axis=0)

    def vectors(low):
        return jnp.concatenate(
            [extra_ref[col, 0, low : low + MINE, :COLS].astype(F32) for col in range(8)], axis=1
        )

    q = vectors(0)
    g = vectors(8)
    channel = lax.broadcasted_iota(jnp.int32, (heads, SINGLE_DIM), 1)
    low = lax.broadcasted_iota(jnp.int32, (heads, SINGLE_DIM), 0) * SINGLE_HEAD_DIM
    inside = (channel >= low) & (channel < low + SINGLE_HEAD_DIM)
    spread = [
        jnp.where(inside, jnp.broadcast_to(q[i : i + 1], (heads, SINGLE_DIM)), 0.0)
        for i in range(MINE)
    ]
    scores = dot(jnp.concatenate(spread, axis=0).astype(BF16), matrix(0)) + bias
    key = lax.broadcasted_iota(jnp.int32, (1, TOKENS), 1)
    scores = jnp.where(key < place_ref[0], scores, MASKED)
    top = jnp.max(scores, axis=1, keepdims=True)
    exponent = jnp.exp2(scores - top)
    total = jnp.sum(exponent, axis=1, keepdims=True)
    mixed = dot_nt((exponent / total).astype(BF16), matrix(1))
    rows = [
        jnp.sum(jnp.where(inside, mixed[heads * i : heads * (i + 1)], 0.0), axis=0, keepdims=True)
        for i in range(MINE)
    ]
    hidden = (g * jnp.concatenate(rows, axis=0)).astype(BF16)
    result = rep_ref[...].astype(F32) + dot(hidden, matrix(2))
    result = jnp.concatenate([result, jnp.zeros((16 - MINE, SINGLE_DIM), F32)], axis=0)
    out_ref[...] = jnp.zeros(out_ref.shape, BF16)
    for col in range(8):
        out_ref[col, 0, :, :COLS] = result[:, COLS * col : COLS * (col + 1)].astype(BF16)


def single_attend(place, early, late, gain, weight, pair, shared, rep):
    shape = (8, 7, 16, CHANNELS)
    last = lambda *_: (0, 6 * MINE, 0, 0)
    return pl.pallas_call(
        single_kernel,
        grid_spec=pltpu.PrefetchScalarGridSpec(
            num_scalar_prefetch=1,
            grid=(1,),
            in_specs=[
                whole((8, 4 * MINE, 16, CHANNELS)),
                whole((8, 2 * MINE + 1, 16, CHANNELS)),
                whole((1, CHANNELS)),
                whole((SINGLE_HEADS, CHANNELS)),
                pl.BlockSpec((8, 1, 16, CHANNELS), last),
            ]
            + [whole(shape)] * 8
            + [whole((MINE, SINGLE_DIM))],
            scratch_shapes=[pltpu.VMEM((2, 4) + shape, BF16)],
            out_specs=pl.BlockSpec((8, 1, 16, CHANNELS), lambda *_: (0, 2 * MINE, 0, 0)),
        ),
        out_shape=jax.ShapeDtypeStruct((8, 2 * MINE + 1, 16, CHANNELS), BF16),
        input_output_aliases={2: 0},
        compiler_params=params(),
        cost_estimate=cost(700),
    )(place, early, late, gain, weight, pair, *shared, rep)


def exchange(value):
    return lax.all_to_all(value, COL, split_axis=0, concat_axis=0, tiled=True)


Z = ("zl", "zh")


def shift(value, axis, by):
    if axis == Z:
        ring = [0, 2, 1, 3]
        pairs = [(ring[i], ring[(i + by) % 4]) for i in range(4)]
    else:
        size = lax.axis_size(axis)
        pairs = [(i, (i + by) % size) for i in range(size)]
    return lax.ppermute(value, axis, pairs)


def around(value, axis):
    return [value, shift(value, axis, -1), shift(value, axis, 2), shift(value, axis, 1)]


def per_device(
    pair_rep,
    single_rep,
    length,
    pair_gain,
    pair_proj,
    bias_weight,
    pair_out_weight,
    single_gain,
    single_proj,
    bias_norm_gain,
    single_bias_weight,
    single_out_weight,
):
    core = lax.axis_index("core")
    x = lax.axis_index("x")
    row = lax.axis_index(ROW)
    col = lax.axis_index(COL)
    second_core = core == 1
    pair_gain = pair_gain.reshape(1, CHANNELS)

    groups = pair_rep.reshape(8, 6 * MINE, 16, CHANNELS)
    limit = length - col * COLS
    bias = local_bias(limit, pair_rep, pair_gain, bias_weight.T)
    kept = lax.dynamic_index_in_dim(bias, core, 0, False)
    given = lax.dynamic_index_in_dim(bias, 1 - core, 0, False)
    taken = shift(given, "core", 1)
    block = jnp.where(second_core, jnp.stack([taken, kept]), jnp.stack([kept, taken]))
    sides = jnp.stack(around(block, "y"))
    after, sides = lax.optimization_barrier((single_rep, sides))
    kv, qg = single_project(
        jnp.stack([row * ROWS, core]),
        after,
        single_gain.reshape(1, SINGLE_DIM),
        jnp.swapaxes(single_proj, 1, 2),
    )
    pieces = around(sides, Z)
    extra = qg.astype(BF16).reshape(2, 8, MINE, COLS)
    extra = jnp.pad(jnp.swapaxes(extra, 0, 1), ((0, 0), (0, 0), (0, 2), (0, CHANNELS - COLS)))
    shared = jnp.concatenate(
        [
            lax.dynamic_index_in_dim(kv, core, 0, False),
            lax.dynamic_slice_in_dim(single_out_weight, core * SINGLE_HEAD_DIM, SINGLE_HEAD_DIM, 0)[None],
        ],
        axis=0,
    )
    shared = jnp.transpose(shared.reshape(3, 3, 16, 3, CHANNELS), (0, 1, 3, 2, 4)).reshape(27, 16, CHANNELS)
    shared = jnp.pad(shared, ((0, 1), (0, 0), (0, 0)))
    shared = lax.dynamic_slice_in_dim(shared, 7 * x, 7, 0)
    message = jnp.concatenate(
        [
            groups,
            extra.reshape(8, 1, 16, CHANNELS),
            jnp.broadcast_to(shared[None], (8, 7, 16, CHANNELS)),
        ],
        axis=1,
    )
    message, pieces = lax.optimization_barrier((message, pieces))
    pair = exchange(message)

    depth = 2 * lax.axis_index("zh") + lax.axis_index("zl")
    own = join(jnp.stack([lax.axis_index("y"), depth]), pieces)
    after = shift(own, "x", -1)
    before = shift(own, "x", 1)
    firsts = [own, after, shift(after[:2], "x", -1), shift(before[2:], "x", 1), before]

    turned = jnp.where(second_core, jnp.roll(pair_proj, 128, axis=2), pair_proj)
    wo = jnp.where(second_core, jnp.roll(pair_out_weight, 128, axis=0), pair_out_weight)
    held = project(pair, pair_gain, turned[0], turned[1].T, turned[2], turned[3])
    seconds = [shift(item, "core", 1) for item in firsts]
    shared = pair[:, 6 * MINE + 1 :]
    shared, _ = lax.optimization_barrier((shared, firsts))
    shared = around(shared, "x")
    swapped = [shift(item, "core", 1) for item in shared]

    x1 = x.reshape(1)
    biases = firsts + seconds
    early = attend(x1, *held, pair, wo, biases, 4, 0, 4 * MINE, 30)
    early, _ = lax.optimization_barrier((early, shared))
    late = attend(x1, *held, pair, wo, biases, 2, 4, 2 * MINE + 1, 16)
    rep = lax.dynamic_slice_in_dim(single_rep, row * ROWS + col * MINE, MINE, 0)
    late = single_attend(
        jnp.concatenate([length, x1, core.reshape(1)]),
        early,
        late,
        bias_norm_gain.reshape(1, CHANNELS),
        single_bias_weight.T,
        pair,
        shared + swapped,
        rep,
    )
    early = exchange(early)
    early, late = lax.optimization_barrier((early, late))
    late = exchange(late)
    single_out = late[:, 2 * MINE, :MINE, :COLS].reshape(ROWS, COLS)
    parts = [early.reshape(8, 4, COLS, CHANNELS), late[:, : 2 * MINE].reshape(8, 2, COLS, CHANNELS)]
    return jnp.concatenate(parts, axis=1).reshape(ROWS, COLS, CHANNELS), single_out


def solution(mesh):
    fine = Mesh(mesh.devices.reshape(4, 2, 2, 4, 2), ROW + COL)
    in_specs = (
        P(ROW, COL, None),
        P(),
        P(),
        P(),
        P(),
        P(),
        P(),
        P(),
        P(None, None, COL),
        P(),
        P(),
        P(COL, None),
    )
    out_specs = (P(ROW, COL, None), P(ROW, COL))
    return jax.shard_map(
        per_device, mesh=fine, in_specs=in_specs, out_specs=out_specs, check_vma=False
    )
```

```python
import functools
import math

import jax
import jax.numpy as jnp
from jax import lax
from jax.experimental import pallas as pl
from jax.experimental.pallas import tpu as pltpu
from jax.sharding import Mesh, PartitionSpec as P

F32 = jnp.float32
BF16 = jnp.bfloat16
TOKENS = 768
CHANNELS = 256
HEADS = 8
HEAD_DIM = 32
SINGLE_DIM = 768
SINGLE_HEADS = 16
SINGLE_HEAD_DIM = 48
ROWS = 48
COLS = 96
MINE = 6
LOG2E = 1.4426950408889634
MASKED = -1e30
ROW = ("x", "zl", "core")
COL = ("y", "zh")
VMEM_LIMIT = 56 * 2**20


def params():
    return pltpu.CompilerParams(vmem_limit_bytes=VMEM_LIMIT)


def cost(time):
    return pl.CostEstimate(flops=time * 10000000, bytes_accessed=time * 30000, transcendentals=0)


def whole(shape):
    zeros = (0,) * len(shape)
    return pl.BlockSpec(shape, lambda *_: zeros)


def normalize(values, scales):
    floated = values.astype(F32)
    center = jnp.mean(floated, axis=-1, keepdims=True)
    moved = floated - center
    spread = jnp.mean(jnp.square(moved), axis=-1, keepdims=True)
    return (moved * lax.rsqrt(spread + 1e-05) * scales).astype(BF16)


def dot(a, b):
    return jnp.dot(a, b, preferred_element_type=F32)


def dot_nt(a, b):
    return lax.dot_general(a, b, (((1,), (1,)), ((), ())), preferred_element_type=F32)


def local_bias_kernel(limit_ref, pair_ref, gain_ref, weight_ref, out_ref, held):
    limit = limit_ref[0]
    key = lax.broadcasted_iota(jnp.int32, (HEADS, COLS), 1)
    weight = weight_ref[...]

    def step(block, carry):
        start = block * 8
        normed = normalize(pair_ref[pl.ds(start, 8)].reshape(8 * COLS, CHANNELS), gain_ref[...])
        bias = dot_nt(weight, normed) * LOG2E
        for row in range(8):
            piece = jnp.where(key < limit, bias[:, row * COLS : (row + 1) * COLS], MASKED)
            held[:, pl.ds(start + row, 1), :] = piece[:, None, :]
        return carry

    lax.fori_loop(0, ROWS // 8, step, 0)
    for half in range(2):
        out_ref[half] = jnp.concatenate([held[4 * half + h] for h in range(4)], axis=1).astype(BF16)


def local_bias(limit, pair, gain, weight):
    return pl.pallas_call(
        local_bias_kernel,
        grid_spec=pltpu.PrefetchScalarGridSpec(
            num_scalar_prefetch=1,
            grid=(1,),
            in_specs=[
                whole((ROWS, COLS, CHANNELS)),
                whole((1, CHANNELS)),
                whole((HEADS, CHANNELS)),
            ],
            out_specs=whole((2, ROWS, 4 * COLS)),
            scratch_shapes=[pltpu.VMEM((HEADS, ROWS, COLS), F32)],
        ),
        out_shape=jax.ShapeDtypeStruct((2, ROWS, 4 * COLS), BF16),
        compiler_params=params(),
        cost_estimate=cost(5),
    )(limit, pair, gain, weight)


def join_kernel(place_ref, a_ref, b_ref, c_ref, d_ref, out_ref, held):
    y = place_ref[0]
    z = place_ref[1]
    for slot, ref in enumerate((a_ref, b_ref, c_ref, d_ref)):
        held[slot] = ref[...]
    for low in range(2):
        for core in range(2):
            blocks = []
            for col in range(8):
                depth = lax.rem(2 * (col % 2) + low - z + 4, 4)
                side = lax.rem(col // 2 - y + 4, 4)
                blocks.append(held[depth, side, core])
            for head in range(4):
                line = jnp.concatenate([b[:, COLS * head : COLS * (head + 1)] for b in blocks], axis=1)
                at = ROWS * (2 * low + core)
                out_ref[head, at : at + ROWS] = line


def join(place, pieces):
    shape = (4, 2, ROWS, 4 * COLS)
    out = (4, 4 * ROWS, TOKENS)
    return pl.pallas_call(
        join_kernel,
        grid_spec=pltpu.PrefetchScalarGridSpec(
            num_scalar_prefetch=1,
            grid=(1,),
            in_specs=[whole(shape)] * 4,
            out_specs=whole(out),
            scratch_shapes=[pltpu.VMEM((4,) + shape, BF16)],
        ),
        out_shape=jax.ShapeDtypeStruct(out, BF16),
        compiler_params=params(),
        cost_estimate=cost(3),
    )(place, *pieces)


def project_kernel(pair_ref, gain_ref, wq_ref, wkt_ref, wv_ref, wg_ref, kt_ref, v_ref, q_ref, g_ref):
    normed = normalize(pair_ref[...].reshape(TOKENS, CHANNELS), gain_ref[...])
    q = (dot(normed, wq_ref[...]) * (LOG2E / math.sqrt(HEAD_DIM))).astype(BF16)
    kt_ref[0] = dot_nt(wkt_ref[...], normed).astype(BF16)
    v_ref[0] = dot(normed, wv_ref[...]).astype(BF16)
    g = jax.nn.sigmoid(dot(normed, wg_ref[...])).astype(BF16)
    q_ref[0] = q.reshape(4, 4 * ROWS, CHANNELS)
    g_ref[0] = g.reshape(4, 4 * ROWS, CHANNELS)


def project(pair, gain, wq, wkt, wv, wg):
    square = whole((CHANNELS, CHANNELS))
    blocks = [(CHANNELS, TOKENS), (TOKENS, CHANNELS)] + [(4, 4 * ROWS, CHANNELS)] * 2

    def spec(block):
        zeros = (0,) * len(block)
        return pl.BlockSpec((1,) + block, lambda i: (i,) + zeros)

    return pl.pallas_call(
        project_kernel,
        grid=(MINE,),
        in_specs=[
            pl.BlockSpec((8, 6, 16, CHANNELS), lambda i: (0, i, 0, 0)),
            whole((1, CHANNELS)),
            square,
            square,
            square,
            square,
        ],
        out_specs=[spec(block) for block in blocks],
        out_shape=[jax.ShapeDtypeStruct((MINE,) + block, BF16) for block in blocks],
        compiler_params=params(),
        cost_estimate=cost(5),
    )(pair, gain, wq, wkt, wv, wg)


def attend_kernel(x_ref, kt_ref, v_ref, q_ref, g_ref, pair_ref, wo_ref, *rest):
    firsts, seconds, out_ref = rest[:5], rest[5:10], rest[10]
    order = [lax.rem(x_ref[0] + step, 4) for step in range(4)]
    span = 4 * ROWS

    def run(exact):
        kt = kt_ref[0]
        v = v_ref[0]
        q = jnp.concatenate([q_ref[0, at] for at in order], axis=0)
        ones = jnp.ones((TOKENS, 128), BF16)
        lane = lax.broadcasted_iota(jnp.int32, (1, CHANNELS), 1)
        half_lane = lax.broadcasted_iota(jnp.int32, (1, 128), 1)
        halves = []
        least = jnp.ones((TOKENS, 128), F32)
        most = least
        for half, refs in enumerate((firsts, seconds)):
            values = jnp.concatenate([v[:, 128 * half : 128 * half + 128], ones], axis=1)
            result = jnp.zeros((TOKENS, 128), F32)
            for head in range(4):
                low = HEAD_DIM * (4 * half + head)
                own = jnp.where((lane >= low) & (lane < low + HEAD_DIM), q, jnp.zeros_like(q))
                low_heads, high_heads = refs[2], refs[3]
                far = low_heads[head] if head < 2 else high_heads[head - 2]
                bias = jnp.concatenate([refs[0][head], refs[1][head], far, refs[4][head]], axis=0)
                scores = dot(own, kt) + bias.astype(F32)
                if exact:
                    scores = scores - jnp.max(scores, axis=1, keepdims=True)
                mixed = dot(jnp.exp2(scores).astype(BF16), values)
                total = mixed[:, 128:]
                least = jnp.minimum(least, total)
                most = jnp.maximum(most, total)
                low = HEAD_DIM * head
                inside = (half_lane >= low) & (half_lane < low + HEAD_DIM)
                result = jnp.where(inside, mixed[:, :128] / total, result)
            halves.append(result)
        attended = jnp.concatenate(halves, axis=1)
        g = jnp.concatenate([g_ref[0, at] for at in order], axis=0)
        update = dot((g.astype(F32) * attended).astype(BF16), wo_ref[...])
        for step, at in enumerate(order):
            old = pair_ref[pl.ds(2 * at, 2)].reshape(span, CHANNELS).astype(F32)
            new = (old + update[span * step : span * (step + 1)]).astype(BF16)
            out_ref[pl.ds(2 * at, 2)] = new.reshape(2, 6, 16, CHANNELS)
        fits = (least > 2.0**-60) & (most < 2.0**100)
        return jnp.min(jnp.where(fits, 1.0, 0.0))

    @pl.when(run(False) < 0.5)
    def _():
        run(True)


def attend(x, kt, v, q, g, pair, wo, biases, rows, start, groups, time):
    def spec(shape):
        zeros = (0,) * len(shape)
        return pl.BlockSpec((1,) + shape, lambda i, x: (start + i,) + zeros)

    parts = spec((4, 4 * ROWS, CHANNELS))
    return pl.pallas_call(
        attend_kernel,
        grid_spec=pltpu.PrefetchScalarGridSpec(
            num_scalar_prefetch=1,
            grid=(rows,),
            in_specs=[
                spec((CHANNELS, TOKENS)),
                spec((TOKENS, CHANNELS)),
                parts,
                parts,
                pl.BlockSpec((8, 6, 16, CHANNELS), lambda i, x: (0, start + i, 0, 0)),
                whole((CHANNELS, CHANNELS)),
            ]
            + [whole(bias.shape) for bias in biases],
            out_specs=pl.BlockSpec((8, 6, 16, CHANNELS), lambda i, x: (0, i, 0, 0)),
        ),
        out_shape=jax.ShapeDtypeStruct((8, groups, 16, CHANNELS), BF16),
        compiler_params=params(),
        cost_estimate=cost(time * 100),
    )(x, kt, v, q, g, pair, wo, *biases)


def single_project_kernel(place_ref, single_ref, gain_ref, weight_ref, kv_ref, qg_ref):
    normed = normalize(single_ref[...], gain_ref[...])
    for kind in range(2):
        both = dot_nt(weight_ref[1 + kind], normed).astype(BF16)
        for head in range(2):
            kv_ref[head, kind] = both[SINGLE_HEAD_DIM * head : SINGLE_HEAD_DIM * (head + 1)]
    start = pl.multiple_of(place_ref[0], 16)
    own = normalize(single_ref[pl.ds(start, ROWS)], gain_ref[...])
    q = dot_nt(own, weight_ref[0]) * (LOG2E / math.sqrt(SINGLE_HEAD_DIM))
    g = jax.nn.sigmoid(dot_nt(own, weight_ref[3]))
    for kind, value in enumerate((q, g)):
        turned = jnp.concatenate([value[:, SINGLE_HEAD_DIM:], value[:, :SINGLE_HEAD_DIM]], axis=1)
        qg_ref[kind] = jnp.where(place_ref[1] == 1, turned, value)


def single_project(place, single, gain, weight):
    return pl.pallas_call(
        single_project_kernel,
        grid_spec=pltpu.PrefetchScalarGridSpec(
            num_scalar_prefetch=1,
            grid=(1,),
            in_specs=[
                whole((TOKENS, SINGLE_DIM)),
                whole((1, SINGLE_DIM)),
                whole((4, COLS, SINGLE_DIM)),
            ],
            out_specs=[whole((2, 2, SINGLE_HEAD_DIM, TOKENS)), whole((2, ROWS, COLS))],
        ),
        out_shape=[
            jax.ShapeDtypeStruct((2, 2, SINGLE_HEAD_DIM, TOKENS), BF16),
            jax.ShapeDtypeStruct((2, ROWS, COLS), F32),
        ],
        compiler_params=params(),
        cost_estimate=cost(4),
    )(place, single, gain, weight)


def single_kernel(
    place_ref, early_ref, late_ref, gain_ref, weight_ref, extra_ref, *rest
):
    heads = SINGLE_HEADS
    shared, rep_ref, out_ref, held = rest[:8], rest[8], rest[9], rest[10]
    for core in range(2):
        for slot in range(4):
            held[core, lax.rem(place_ref[1] + slot, 4)] = shared[4 * core + slot][...]
    weight = weight_ref[...].astype(F32)
    line = lax.broadcasted_iota(jnp.int32, weight.shape, 0)
    turned = jnp.where(line % 2 == 0, pltpu.roll(weight, heads - 1, 0), pltpu.roll(weight, 1, 0))
    weight = jnp.where(place_ref[2] == 1, turned, weight).astype(BF16)
    biases = []
    for i in range(MINE):
        tokens = early_ref[:, 6 * i : 6 * i + 6] if i < 4 else late_ref[:, 6 * i - 24 : 6 * i - 18]
        normed = normalize(tokens.reshape(TOKENS, CHANNELS), gain_ref[...])
        biases.append(dot_nt(weight, normed).astype(BF16).astype(F32))
    bias = jnp.concatenate(biases, axis=0) * LOG2E

    def piece(core, col, kind, band, third):
        at = 9 * kind + 3 * band + third
        return held[core, at // 7, col, at % 7]

    def matrix(kind):
        rows = []
        for col in range(8):
            for core in range(2):
                for band in range(3):
                    rows.append(
                        jnp.concatenate([piece(core, col, kind, band, third) for third in range(3)], axis=1)
                    )
        return jnp.concatenate(rows, axis=0)

    def vectors(low):
        return jnp.concatenate(
            [extra_ref[col, 0, low : low + MINE, :COLS].astype(F32) for col in range(8)], axis=1
        )

    q = vectors(0)
    g = vectors(8)
    channel = lax.broadcasted_iota(jnp.int32, (heads, SINGLE_DIM), 1)
    low = lax.broadcasted_iota(jnp.int32, (heads, SINGLE_DIM), 0) * SINGLE_HEAD_DIM
    inside = (channel >= low) & (channel < low + SINGLE_HEAD_DIM)
    spread = [
        jnp.where(inside, jnp.broadcast_to(q[i : i + 1], (heads, SINGLE_DIM)), 0.0)
        for i in range(MINE)
    ]
    scores = dot(jnp.concatenate(spread, axis=0).astype(BF16), matrix(0)) + bias
    key = lax.broadcasted_iota(jnp.int32, (1, TOKENS), 1)
    scores = jnp.where(key < place_ref[0], scores, MASKED)
    top = jnp.max(scores, axis=1, keepdims=True)
    exponent = jnp.exp2(scores - top)
    total = jnp.sum(exponent, axis=1, keepdims=True)
    mixed = dot_nt((exponent / total).astype(BF16), matrix(1))
    rows = [
        jnp.sum(jnp.where(inside, mixed[heads * i : heads * (i + 1)], 0.0), axis=0, keepdims=True)
        for i in range(MINE)
    ]
    hidden = (g * jnp.concatenate(rows, axis=0)).astype(BF16)
    result = rep_ref[...].astype(F32) + dot(hidden, matrix(2))
    result = jnp.concatenate([result, jnp.zeros((16 - MINE, SINGLE_DIM), F32)], axis=0)
    out_ref[...] = jnp.zeros(out_ref.shape, BF16)
    for col in range(8):
        out_ref[col, 0, :, :COLS] = result[:, COLS * col : COLS * (col + 1)].astype(BF16)


def single_attend(place, early, late, gain, weight, pair, shared, rep):
    shape = (8, 7, 16, CHANNELS)
    last = lambda *_: (0, 6 * MINE, 0, 0)
    return pl.pallas_call(
        single_kernel,
        grid_spec=pltpu.PrefetchScalarGridSpec(
            num_scalar_prefetch=1,
            grid=(1,),
            in_specs=[
                whole((8, 4 * MINE, 16, CHANNELS)),
                whole((8, 2 * MINE + 1, 16, CHANNELS)),
                whole((1, CHANNELS)),
                whole((SINGLE_HEADS, CHANNELS)),
                pl.BlockSpec((8, 1, 16, CHANNELS), last),
            ]
            + [whole(shape)] * 8
            + [whole((MINE, SINGLE_DIM))],
            scratch_shapes=[pltpu.VMEM((2, 4) + shape, BF16)],
            out_specs=pl.BlockSpec((8, 1, 16, CHANNELS), lambda *_: (0, 2 * MINE, 0, 0)),
        ),
        out_shape=jax.ShapeDtypeStruct((8, 2 * MINE + 1, 16, CHANNELS), BF16),
        input_output_aliases={2: 0},
        compiler_params=params(),
        cost_estimate=cost(700),
    )(place, early, late, gain, weight, pair, *shared, rep)


def exchange(value):
    return lax.all_to_all(value, COL, split_axis=0, concat_axis=0, tiled=True)


Z = ("zl", "zh")


def shift(value, axis, by):
    if axis == Z:
        ring = [0, 2, 1, 3]
        pairs = [(ring[i], ring[(i + by) % 4]) for i in range(4)]
    else:
        size = lax.axis_size(axis)
        pairs = [(i, (i + by) % size) for i in range(size)]
    return lax.ppermute(value, axis, pairs)


def around(value, axis):
    return [value, shift(value, axis, -1), shift(value, axis, 2), shift(value, axis, 1)]


def per_device(
    pair_rep,
    single_rep,
    length,
    pair_gain,
    pair_proj,
    bias_weight,
    pair_out_weight,
    single_gain,
    single_proj,
    bias_norm_gain,
    single_bias_weight,
    single_out_weight,
):
    core = lax.axis_index("core")
    x = lax.axis_index("x")
    row = lax.axis_index(ROW)
    col = lax.axis_index(COL)
    second_core = core == 1
    pair_gain = pair_gain.reshape(1, CHANNELS)

    groups = pair_rep.reshape(8, 6 * MINE, 16, CHANNELS)
    limit = length - col * COLS
    bias = local_bias(limit, pair_rep, pair_gain, bias_weight.T)
    kept = lax.dynamic_index_in_dim(bias, core, 0, False)
    given = lax.dynamic_index_in_dim(bias, 1 - core, 0, False)
    taken = shift(given, "core", 1)
    block = jnp.where(second_core, jnp.stack([taken, kept]), jnp.stack([kept, taken]))
    sides = jnp.stack(around(block, "y"))
    after, sides = lax.optimization_barrier((single_rep, sides))
    kv, qg = single_project(
        jnp.stack([row * ROWS, core]),
        after,
        single_gain.reshape(1, SINGLE_DIM),
        jnp.swapaxes(single_proj, 1, 2),
    )
    pieces = around(sides, Z)
    extra = qg.astype(BF16).reshape(2, 8, MINE, COLS)
    extra = jnp.pad(jnp.swapaxes(extra, 0, 1), ((0, 0), (0, 0), (0, 2), (0, CHANNELS - COLS)))
    shared = jnp.concatenate(
        [
            lax.dynamic_index_in_dim(kv, core, 0, False),
            lax.dynamic_slice_in_dim(single_out_weight, core * SINGLE_HEAD_DIM, SINGLE_HEAD_DIM, 0)[None],
        ],
        axis=0,
    )
    shared = jnp.transpose(shared.reshape(3, 3, 16, 3, CHANNELS), (0, 1, 3, 2, 4)).reshape(27, 16, CHANNELS)
    shared = jnp.pad(shared, ((0, 1), (0, 0), (0, 0)))
    shared = lax.dynamic_slice_in_dim(shared, 7 * x, 7, 0)
    message = jnp.concatenate(
        [
            groups,
            extra.reshape(8, 1, 16, CHANNELS),
            jnp.broadcast_to(shared[None], (8, 7, 16, CHANNELS)),
        ],
        axis=1,
    )
    message, pieces = lax.optimization_barrier((message, pieces))
    pair = exchange(message)

    depth = 2 * lax.axis_index("zh") + lax.axis_index("zl")
    own = join(jnp.stack([lax.axis_index("y"), depth]), pieces)
    after = shift(own, "x", -1)
    before = shift(own, "x", 1)
    firsts = [own, after, shift(after[:2], "x", -1), shift(before[2:], "x", 1), before]

    turned = jnp.where(second_core, jnp.roll(pair_proj, 128, axis=2), pair_proj)
    wo = jnp.where(second_core, jnp.roll(pair_out_weight, 128, axis=0), pair_out_weight)
    held = project(pair, pair_gain, turned[0], turned[1].T, turned[2], turned[3])
    seconds = [shift(item, "core", 1) for item in firsts]
    shared = pair[:, 6 * MINE + 1 :]
    shared, _ = lax.optimization_barrier((shared, firsts))
    shared = around(shared, "x")
    swapped = [shift(item, "core", 1) for item in shared]

    x1 = x.reshape(1)
    biases = firsts + seconds
    early = attend(x1, *held, pair, wo, biases, 4, 0, 4 * MINE, 30)
    early, _ = lax.optimization_barrier((early, shared))
    late = attend(x1, *held, pair, wo, biases, 2, 4, 2 * MINE + 1, 16)
    rep = lax.dynamic_slice_in_dim(single_rep, row * ROWS + col * MINE, MINE, 0)
    late = single_attend(
        jnp.concatenate([length, x1, core.reshape(1)]),
        early,
        late,
        bias_norm_gain.reshape(1, CHANNELS),
        single_bias_weight.T,
        pair,
        shared + swapped,
        rep,
    )
    early = exchange(early)
    early, late = lax.optimization_barrier((early, late))
    late = exchange(late)
    single_out = late[:, 2 * MINE, :MINE, :COLS].reshape(ROWS, COLS)
    parts = [early.reshape(8, 4, COLS, CHANNELS), late[:, : 2 * MINE].reshape(8, 2, COLS, CHANNELS)]
    return jnp.concatenate(parts, axis=1).reshape(ROWS, COLS, CHANNELS), single_out


def solution(mesh):
    fine = Mesh(mesh.devices.reshape(4, 2, 2, 4, 2), ROW + COL)
    in_specs = (
        P(ROW, COL, None),
        P(),
        P(),
        P(),
        P(),
        P(),
        P(),
        P(),
        P(None, None, COL),
        P(),
        P(),
        P(COL, None),
    )
    out_specs = (P(ROW, COL, None), P(ROW, COL))
    return jax.shard_map(
        per_device, mesh=fine, in_specs=in_specs, out_specs=out_specs, check_vma=False
    )
```
